128 devices in a mesh: dp: 8 (over y, core), fsdp: 16 (over z, x).
Axes of the slice: x: 4, y: 4, z: 4, core: 2. Of those that a mesh axis runs over, the one named last changes fastest.
Arguments:
- data_samples: bfloat16 [1024, 4096], P('dp', 'fsdp'), may hold values from -6 to 6
- negative_start: float32 [1024, 4096], P('dp', 'fsdp'), may hold values from -6 to 6
- langevin_noise: float32 [4, 1024, 4096], P(None, 'dp', 'fsdp'), may hold values from -6 to 6
- first_weight: bfloat16 [4096, 4096], P('fsdp'), may hold values from -0.09375 to 0.09375
- second_weight: bfloat16 [4096, 4096], P('fsdp'), may hold values from -0.09375 to 0.09375
- readout: float32 [4096], P('fsdp'), may hold values from -480 to 480
Outputs:
- first_grad: float32 [4096, 4096], P('fsdp', 'dp')
- second_grad: float32 [4096, 4096], P('fsdp', 'dp')
- energy_gap: float32 [], replicated
The draws below stay inside these ranges and needn't reach their ends.
All inputs are finite; a program needn't handle non-finite values.
Results may differ from the reference program's by a relative error of at most 0.014.
Values may be sent and summed in bfloat16 or wider, within the bound.
No kernel may reach another device: no remote copies, remote signals or barrier semaphores. Data moves between devices by JAX's collectives and lax.ppermute only.
A program may use at most 64 MiB of HBM per device.

```python
import jax
import jax.numpy as jnp
from jax import lax

D = 4096
H = 4096
STEPS = 4
SAMPLES = 1024
N_FSDP = 16


def levels(own_key, shape, cuts, least, high):
    level = 1.0
    for axis_at, shards_of in cuts:
        heights = jax.random.uniform(jax.random.fold_in(jax.random.fold_in(own_key, 6), axis_at), (shards_of,), jnp.float32, least / len(cuts), high / len(cuts))
        level = level * jnp.repeat(jnp.exp(heights), shape[axis_at] // shards_of).reshape((-1,) + (1,) * (len(shape) - 1 - axis_at))
    return level


def bell_draw(rng, extent, spread, most, cuts=(), kind=jnp.bfloat16):
    entries = jax.random.normal(rng, extent, jnp.float32) * spread
    if len(cuts) > 0:
        entries = levels(rng, extent, cuts, -0.22, 0.18) * entries
    return jnp.clip(entries, min=-most, max=most).astype(kind)


def setup_inputs(seed: int = 0) -> dict:
    arg_keys = jax.random.split(jax.random.key(seed), 7)
    return {
        "data_samples": bell_draw(arg_keys[0], (SAMPLES, D), 1.0, 6.0, ((0, 8), (1, 16))),
        "negative_start": bell_draw(arg_keys[1], (SAMPLES, D), 1.0, 6.0, ((0, 8), (1, 16)), jnp.float32),
        "langevin_noise": bell_draw(arg_keys[2], (STEPS, SAMPLES, D), 1.0, 6.0, ((1, 8), (2, 16)), jnp.float32),
        "first_weight": bell_draw(arg_keys[3], (D, H), D ** -0.5, 0.09375, ((0, 16),)),
        "second_weight": bell_draw(arg_keys[4], (H, H), H ** -0.5, 0.09375, ((0, 16),)),
        "readout": bell_draw(arg_keys[5], (H,), 80.0, 480.0, ((0, 16),), jnp.float32),
    }


def slope(values):
    sig = jax.nn.sigmoid(values)
    return sig * (1.0 + values * (1.0 - sig))

def layer(inputs, weight):
    count = inputs.shape[0]
    width = weight.shape[0]
    pieces = jnp.einsum('rnk,nkh->nrh', inputs.reshape(count, N_FSDP, width // N_FSDP).astype(jnp.float32), weight.reshape(N_FSDP, width // N_FSDP, weight.shape[1]).astype(jnp.float32), precision=lax.Precision.HIGHEST)
    rounded = lax.optimization_barrier(pieces.astype(jnp.bfloat16))
    return lax.optimization_barrier(jnp.sum(rounded.astype(jnp.float32), axis=0))

def forward(inputs, first_weight, second_weight):
    pre_one = layer(inputs, first_weight)
    hidden = jax.nn.silu(pre_one).astype(jnp.bfloat16)
    pre_two = layer(hidden, second_weight)
    return (pre_one, hidden, pre_two)

def backward(cotan, readout, pre_one, pre_two, second_weight):
    grad_two = (cotan[:, None] * readout[None, :] * slope(pre_two)).astype(jnp.bfloat16)
    back_one = jnp.dot(grad_two, second_weight.T, preferred_element_type=jnp.float32)
    grad_one = (back_one * slope(pre_one)).astype(jnp.bfloat16)
    return (grad_two, grad_one)

def reference(data_samples, negative_start, langevin_noise, first_weight, second_weight, readout):
    state = negative_start
    ones = jnp.ones((state.shape[0],), jnp.float32)
    for step in range(STEPS):
        inputs = state.astype(jnp.bfloat16)
        pre_one, hidden, pre_two = forward(inputs, first_weight, second_weight)
        grad_two, grad_one = backward(ones, readout, pre_one, pre_two, second_weight)
        moved = jnp.dot(grad_one, first_weight.T, preferred_element_type=jnp.float32)
        state = state - 0.005 * moved + 0.1 * langevin_noise[step]
    rows = jnp.concatenate([data_samples, state.astype(jnp.bfloat16)], axis=0)
    cotan = jnp.concatenate([ones, -ones])
    pre_one, hidden, pre_two = forward(rows, first_weight, second_weight)
    energies = jnp.dot(jax.nn.silu(pre_two), readout, precision=lax.Precision.HIGHEST)
    energy_gap = jnp.sum(cotan * energies) / (SAMPLES * 80.0 * jnp.sqrt(jnp.float32(H)))
    grad_two, grad_one = backward(cotan, readout, pre_one, pre_two, second_weight)
    raw_one = jnp.dot(rows.T, grad_one, preferred_element_type=jnp.float32)
    raw_two = jnp.dot(hidden.T, grad_two, preferred_element_type=jnp.float32)
    total = jnp.sum(raw_one * raw_one) + jnp.sum(raw_two * raw_two)
    scale = jnp.sqrt(total / (2.0 * D * H) + 1e-06)
    return (raw_one / scale, raw_two / scale, energy_gap)
```

```python
import jax
import jax.numpy as jnp
from jax import lax
from jax.sharding import Mesh
from jax.sharding import PartitionSpec as P

STEPS = 4
AXES = ("y", "c", "z", "a", "b")
DP = ("y", "c")
ZA = ("z", "a")
FSDP = ("z", "a", "b")
SWAP = [(0, 1), (1, 0)]
UP = [(0, 1), (1, 2), (2, 3), (3, 0)]
DOWN = [(0, 3), (1, 0), (2, 1), (3, 2)]
OVER = [(0, 2), (1, 3), (2, 0), (3, 1)]


def pick(value, index, dim):
    return lax.dynamic_index_in_dim(value, index, dim, keepdims=False)


def swap(value, axis):
    return lax.ppermute(value, axis, SWAP)


def put(buffer, piece, starts):
    starts = tuple(starts) + (0,) * (buffer.ndim - len(starts))
    return lax.dynamic_update_slice(buffer, piece, starts)


def ring_bulk(piece, axis):
    half = piece.shape[-2] // 2
    from_low = lax.ppermute(piece, axis, UP)
    from_high = lax.ppermute(piece, axis, DOWN)
    far_a = lax.ppermute(from_low[..., :half, :], axis, UP)
    far_b = lax.ppermute(from_high[..., half:, :], axis, DOWN)
    far = jnp.concatenate([far_a, far_b], axis=-2)
    return (piece, from_low, from_high, far)


def ring_order(axis):
    me = lax.axis_index(axis)
    return (me, (me + 3) % 4, (me + 1) % 4, (me + 2) % 4)


def gather_first(weight, c, b):
    rows, cols = weight.shape
    unit = cols // 16
    a = lax.axis_index("a")
    piece = pick(weight.reshape(rows, 8, 2, unit), c, 2).reshape(rows, 8 * unit)
    across = swap(piece, "a")
    out = jnp.zeros((4, 2, rows, 8 * unit), weight.dtype)
    for value, at in ((piece, a), (across, 1 - a)):
        for part, z in zip(ring_bulk(value, "z"), ring_order("z")):
            out = put(out, part[None, None], (z, at))
    return out.reshape(8, rows, 8 * unit)


def gather_second(weight, c, b):
    rows, cols = weight.shape
    unit = cols // 16
    part = rows // 4
    y, a = lax.axis_index("y"), lax.axis_index("a")
    mine = lax.dynamic_slice_in_dim(weight, y * part, part, 0).reshape(part, 8, 2, unit)
    theirs = swap(pick(mine, 1 - b, 2), "b")
    piece = jnp.where(c == b, pick(mine, b, 2), theirs).reshape(part, 8 * unit)
    across = swap(piece, "a")
    both = jnp.where(a == 0, jnp.stack([piece, across]), jnp.stack([across, piece]))
    column = jnp.zeros((4, 2, part, 8 * unit), weight.dtype)
    moves = (both, *(lax.ppermute(both, "z", way) for way in (UP, DOWN, OVER)))
    for value, z in zip(moves, ring_order("z")):
        column = put(column, value[None], (z,))
    out = jnp.zeros((4, 2, 4, part, 8 * unit), weight.dtype)
    for value, at in zip(ring_bulk(column, "y"), ring_order("y")):
        out = put(out, value[:, :, None], (0, 0, at))
    return out.reshape(8, rows, 8 * unit)


def to_groups(value):
    lead, rows, cols = value.shape
    part = rows // 8
    split = jnp.moveaxis(value.reshape(lead, 8, part, cols), 1, 0)
    got = lax.all_to_all(split, ZA, 0, 0, tiled=True)
    own = jnp.transpose(got, (1, 2, 0, 3)).reshape(lead, part, 8 * cols)
    other = swap(own, "c")
    first = lax.axis_index("c") == 0
    return jnp.concatenate([jnp.where(first, own, other), jnp.where(first, other, own)], axis=1)


def spread(value, axis):
    count = lax.axis_size(axis)
    return lax.all_to_all(jnp.broadcast_to(value, (count, *value.shape)), axis, 0, 0, tiled=True)


def slope(values):
    sig = jax.nn.sigmoid(values)
    return sig * (1.0 + values * (1.0 - sig))


def share(part, axis):
    return part + swap(part, axis)


def layer(inputs, block, axis):
    slices, depth, _ = block.shape
    split = inputs.reshape(inputs.shape[0], slices, depth)
    terms = jnp.einsum("rnk,nkm->nrm", split, block, preferred_element_type=jnp.float32)
    part = jnp.sum(terms.astype(jnp.bfloat16).astype(jnp.float32), axis=0)
    return share(part, axis)


def back(cotan, block, axis):
    flat = block.reshape(-1, block.shape[-1])
    part = lax.dot_general(
        cotan, flat, (((1,), (1,)), ((), ())), preferred_element_type=jnp.float32
    )
    return share(part, axis)


def one_pass(inputs, cotan, readout, first, second):
    pre_one = layer(inputs, first, "b")
    hidden = jax.nn.silu(pre_one).astype(jnp.bfloat16)
    pre_two = layer(hidden, second, "c")
    grad_two = (cotan[:, None] * readout[None, :] * slope(pre_two)).astype(jnp.bfloat16)
    grad_one = (back(grad_two, second, "b") * slope(pre_one)).astype(jnp.bfloat16)
    return (hidden, pre_two, grad_two, grad_one)


def local(data_samples, negative_start, langevin_noise, first_weight, second_weight, readout):
    c, b = lax.axis_index("c"), lax.axis_index("b")
    first = gather_first(first_weight, c, b)
    second = gather_second(second_weight, c, b)
    moved_in = to_groups(jnp.concatenate([negative_start[None], langevin_noise]))
    data = to_groups(data_samples[None])[0]
    state, noise = (moved_in[0], moved_in[1:])
    readout = spread(readout, ZA).reshape(-1)
    count = state.shape[0]
    ones = jnp.ones((count,), jnp.float32)
    for step in range(STEPS):
        inputs = state.astype(jnp.bfloat16)
        _, _, _, grad_one = one_pass(inputs, ones, readout, first, second)
        state = state - 0.005 * back(grad_one, first, "c") + 0.1 * noise[step]
    rows = jnp.concatenate([data, state.astype(jnp.bfloat16)], axis=0)
    cotan = jnp.concatenate([ones, -ones])
    hidden, pre_two, grad_two, grad_one = one_pass(rows, cotan, readout, first, second)
    energies = jnp.sum(jax.nn.silu(pre_two) * readout[None, :], axis=1)
    signed = 0.5 * jnp.sum(cotan * energies)

    unit = rows.shape[1] // 8
    half = lambda value, at: pick(value.reshape(2, count, 8, unit), at, 0)
    crossed = swap(half(hidden, 1 - c), "c")
    hidden_part = jnp.where(c == b, half(hidden, c), crossed)
    inner = jnp.stack([half(rows, c), hidden_part])
    inner = lax.all_to_all(jnp.moveaxis(inner, 2, 0), ZA, 0, 0, tiled=True)
    inner = lax.all_gather(inner, DP, axis=0)
    outer_two = lax.all_to_all(jnp.moveaxis(half(grad_two, c), 1, 0), DP, 0, 0, tiled=True)
    outer_one = lax.all_to_all(jnp.moveaxis(half(grad_one, b), 1, 0), DP, 0, 0, tiled=True)
    outer_two = spread(outer_two, FSDP).reshape(4, 2, 2, 4, 2, count, unit)
    outer_one = spread(outer_one, FSDP).reshape(4, 2, 2, 4, 2, count, unit)
    inner = inner.reshape(4, 2, 4, 2, 2, count, unit)
    raw_one = jnp.einsum(
        "yhzark,zahytrm->ktm", inner[:, :, :, :, 0], outer_one, preferred_element_type=jnp.float32
    ).reshape(unit, 2 * unit)
    raw_two = jnp.einsum(
        "yhzark,zatyhrm->ktm", inner[:, :, :, :, 1], outer_two, preferred_element_type=jnp.float32
    ).reshape(unit, 2 * unit)
    squares = jnp.sum(raw_one * raw_one) + jnp.sum(raw_two * raw_two)
    sums = jnp.stack([signed, squares])
    for axes in ("c", "y", "z", ("a", "b")):
        sums = lax.psum(sums, axes)
    width = 16 * unit
    energy_gap = sums[0] / (count * 32 * 80.0 * jnp.sqrt(jnp.float32(width)))
    scale = jnp.sqrt(sums[1] / (2.0 * width * width) + 1e-06)
    return (raw_one / scale, raw_two / scale, energy_gap)


def solution(mesh):
    split = Mesh(mesh.devices.reshape(4, 2, 4, 2, 2), AXES)
    in_specs = (
        P(DP, FSDP), P(DP, FSDP), P(None, DP, FSDP), P(FSDP, None), P(FSDP, None), P(FSDP),
    )
    out_specs = (P(FSDP, DP), P(FSDP, DP), P())
    return jax.shard_map(local, mesh=split, in_specs=in_specs, out_specs=out_specs, check_vma=False)
```

```python
import jax
import jax.numpy as jnp
from jax import lax
from jax.experimental import pallas as pl
from jax.experimental.pallas import tpu as pltpu
from jax.sharding import Mesh
from jax.sharding import PartitionSpec as P

STEPS = 4
AXES = ("y", "c", "z", "a", "b")
DP = ("y", "c")
ZA = ("z", "a")
FSDP = ("z", "a", "b")
X = ("a", "b")


def pick(value, index, dim):
    return lax.dynamic_index_in_dim(value, index, dim, keepdims=False)


def send(value, axis, step):
    count = lax.axis_size(axis)
    return lax.ppermute(value, axis, [(j, j ^ step) for j in range(count)])


def swap(value, axis):
    return send(value, axis, 1)


def from_all(value, axis):
    near = {step: send(value, axis, step) for step in (1, 3, 2)}
    return [value, near[1], near[2], near[3]]


def to_each(values, axis):
    near = {step: send(values[step], axis, step) for step in (1, 3, 2)}
    return [values[0], near[1], near[2], near[3]]


def total(value, axis):
    parts = from_all(value, axis)
    return (parts[0] + parts[1]) + (parts[2] + parts[3])


def relative(value, axis, dim):
    me = lax.axis_index(axis)
    return jnp.stack([pick(value, me ^ k, dim) for k in range(value.shape[dim])], axis=dim)


def put(buffer, piece, starts):
    starts = tuple(starts) + (0,) * (buffer.ndim - len(starts))
    return lax.dynamic_update_slice(buffer, piece, starts)


def both_ways(left, right, axis):
    left_one, right_three = send(left, axis, 1), send(right, axis, 3)
    left_three, right_one = send(left, axis, 3), send(right, axis, 1)
    left_two = send(left_one, axis, 3)
    right_two = send(right_three, axis, 1)
    return ([left, left_one, left_two, left_three], [right, right_one, right_two, right_three])


def gather_second_column(weight, c, b):
    rows, cols = weight.shape
    unit = cols // 16
    part = rows // 4
    y = lax.axis_index("y")
    mine = lax.dynamic_slice_in_dim(weight, y * part, part, 0).reshape(part, 8, 2, unit)
    theirs = swap(pick(mine, 1 - b, 2).reshape(part, 8 * unit), "b")
    piece = jnp.where(c == b, pick(mine, b, 2).reshape(part, 8 * unit), theirs)
    across = swap(piece, "a")
    return both_ways(piece, across, "z")


def gather_second(column):
    part, width = column[0][0].shape
    me = {axis: lax.axis_index(axis) for axis in ("y", "z", "a")}
    stacks = [jnp.concatenate(pieces, axis=0) for pieces in column]
    moved = both_ways(*stacks, "y")
    out = jnp.zeros((4, 2, 4, part, width), column[0][0].dtype)
    for ky in (0, 1, 3, 2):
        for ka in (0, 1):
            pieces = moved[ka][ky].reshape(4, 1, 1, part, width)
            for kz in range(4):
                out = put(
                    out, pieces[kz : kz + 1], (me["z"] ^ kz, me["a"] ^ ka, me["y"] ^ ky)
                )
    return out.reshape(8, 4 * part, width)


def first_piece(weight, c):
    rows, cols = weight.shape
    unit = cols // 16
    piece = pick(weight.reshape(rows, 8, 2, unit), c, 2).reshape(rows, 8 * unit)
    return (piece, swap(piece, "a"))


def gather_first(piece, across):
    own, other = both_ways(piece, across, "z")
    return jnp.stack([part for pair in zip(own, other) for part in pair])


def to_groups(value):
    lead, rows, cols = value.shape
    part = rows // 8
    split = jnp.moveaxis(value.reshape(lead, 8, part, cols), 1, 0)
    got = lax.all_to_all(split, ZA, 0, 0, tiled=True).reshape(4, 2, lead, part, cols)
    got = relative(relative(got, "z", 0), "a", 1).reshape(8, lead, part, cols)
    own = jnp.transpose(got, (1, 2, 0, 3)).reshape(lead, part, 8 * cols)
    return by_index("c", own, swap(own, "c"), 1)


def by_index(axis, own, other, dim):
    first = lax.axis_index(axis) == 0
    return jnp.concatenate(
        [jnp.where(first, own, other), jnp.where(first, other, own)], axis=dim
    )


def spread(value, axis):
    count = lax.axis_size(axis)
    return lax.all_to_all(jnp.broadcast_to(value, (count, *value.shape)), axis, 0, 0, tiled=True)


def slope(values):
    sig = jax.nn.sigmoid(values)
    return sig * (1.0 + values * (1.0 - sig))


def share(part, axis, narrow):
    if narrow and axis == "b":
        part = part.astype(jnp.bfloat16)
    return part.astype(jnp.float32) + swap(part, axis).astype(jnp.float32)


def layer(inputs, block, axis, narrow):
    slices, depth, _ = block.shape
    split = inputs.reshape(inputs.shape[0], slices, depth)
    terms = jnp.einsum("rnk,nkm->nrm", split, block, preferred_element_type=jnp.float32)
    part = jnp.sum(terms.astype(jnp.bfloat16).astype(jnp.float32), axis=0)
    return share(part, axis, narrow)


def back(cotan, block, axis, narrow):
    flat = block.reshape(-1, block.shape[-1])
    part = lax.dot_general(
        cotan, flat, (((1,), (1,)), ((), ())), preferred_element_type=jnp.float32
    )
    return share(part, axis, narrow)


def one_pass(inputs, cotan, readout, first, second, narrow):
    pre_one = layer(inputs, first, "b", narrow)
    hidden = jax.nn.silu(pre_one).astype(jnp.bfloat16)
    pre_two = layer(hidden, second, "c", narrow)
    grad_two = (cotan[:, None] * readout[None, :] * slope(pre_two)).astype(jnp.bfloat16)
    grad_one = (back(grad_two, second, "b", narrow) * slope(pre_one)).astype(jnp.bfloat16)
    return (hidden, pre_two, grad_two, grad_one)


def products(u_ref, g_ref, h_ref, q_ref, one_ref, two_ref, sum_ref):
    one = jnp.dot(u_ref[...], g_ref[...], preferred_element_type=jnp.float32)
    one_ref[...] = one
    two = jnp.dot(h_ref[...], q_ref[...], preferred_element_type=jnp.float32)
    two_ref[...] = two
    sum_ref[...] = jnp.full(sum_ref.shape, jnp.sum(one * one) + jnp.sum(two * two))


def contract(u, g, h, q):
    tile = jax.ShapeDtypeStruct((u.shape[0], g.shape[1]), jnp.float32)
    return pl.pallas_call(
        products,
        out_shape=(tile, tile, jax.ShapeDtypeStruct((8, 128), jnp.float32)),
        compiler_params=pltpu.CompilerParams(vmem_limit_bytes=32 * 1024 * 1024),
    )(u, g, h, q)


def rows_to_owner(rows, hidden, c, b):
    count = rows.shape[0] // 2
    unit = rows.shape[1] // 8
    half = lambda value, at: pick(value.reshape(2, count, 4, 2, unit), at, 0)
    crossed = swap(half(hidden, 1 - c), "c")
    hidden_part = jnp.where(c == b, half(hidden, c), crossed)
    hidden_part = relative(relative(hidden_part, "z", 1), "a", 2)
    parts = jnp.concatenate([half(rows, c), hidden_part], axis=-1)
    parts = jnp.transpose(parts, (2, 1, 0, 3))
    pairs = jnp.stack([parts[0], swap(parts[1], "a")], axis=1)
    column = jnp.stack(to_each([pairs[k] for k in range(4)], "z"))
    plane = jnp.stack(from_all(column, "y"))
    return by_index("c", plane[None], swap(plane, "c")[None], 0)


def second_to_owner(grad, c):
    count = grad.shape[0] // 2
    unit = grad.shape[1] // 8
    mine = pick(grad.reshape(2, count, 4, 2, unit), c, 0)
    parts = jnp.transpose(relative(relative(mine, "y", 1), "c", 2), (2, 1, 0, 3))
    pairs = by_index("c", parts[0][:, None], swap(parts[1], "c")[:, None], 1)
    block = jnp.stack(to_each([pairs[k] for k in range(4)], "y"))
    near = from_all(block, X)
    row = jnp.stack([by_index("b", near[2 * k], near[2 * k + 1], -1) for k in range(2)])
    return jnp.stack(from_all(row, "z")).reshape(-1, 2 * unit)


def first_to_owner(grad, b):
    count = grad.shape[0] // 2
    unit = grad.shape[1] // 8
    mine = pick(grad.reshape(2, count, 4, 2, unit), b, 0)
    parts = jnp.transpose(relative(relative(mine, "y", 1), "c", 2), (2, 1, 0, 3))
    pairs = by_index("c", parts[0], swap(parts[1], "c"), -1)
    block = jnp.stack(to_each([pairs[k] for k in range(4)], "y"))
    column = jnp.stack(from_all(block, "z"))
    near = from_all(column, X)
    return jnp.stack(
        [by_index("b", near[2 * k][None], near[2 * k + 1][None], 0) for k in range(2)]
    ).reshape(-1, 2 * unit)


def local(data_samples, negative_start, langevin_noise, first_weight, second_weight, readout):
    c, b = lax.axis_index("c"), lax.axis_index("b")
    column = gather_second_column(second_weight, c, b)
    piece, across = first_piece(first_weight, c)
    tied = lax.optimization_barrier((piece, across, column[0][1], column[1][3]))
    piece, across = tied[:2]
    column[0][1], column[1][3] = tied[2:]
    first = gather_first(piece, across)
    start = jnp.concatenate([negative_start[None], langevin_noise])
    start, data, readout, column = lax.optimization_barrier(
        (start, data_samples[None], readout, column)
    )
    second = gather_second(column)
    moved_in = to_groups(start)
    data = to_groups(data)[0]
    state, noise = (moved_in[0], moved_in[1:])
    readout = spread(readout, ZA).reshape(-1)
    count = state.shape[0]
    ones = jnp.ones((count,), jnp.float32)
    for step in range(STEPS):
        inputs = state.astype(jnp.bfloat16)
        grad_one = one_pass(inputs, ones, readout, first, second, True)[3]
        state = state - 0.005 * back(grad_one, first, "c", True) + 0.1 * noise[step]
    rows = jnp.concatenate([data, state.astype(jnp.bfloat16)], axis=0)
    cotan = jnp.concatenate([ones, -ones])
    hidden, pre_two, grad_two, grad_one = one_pass(rows, cotan, readout, first, second, False)
    energies = jnp.sum(jax.nn.silu(pre_two) * readout[None, :], axis=1)
    signed = 0.5 * jnp.sum(cotan * energies)

    unit = rows.shape[1] // 8
    inner = rows_to_owner(rows, hidden, c, b)
    u = jnp.transpose(inner[..., :unit], (5, 3, 0, 2, 1, 4)).reshape(unit, -1)
    h = jnp.transpose(inner[..., unit:], (5, 2, 3, 1, 0, 4)).reshape(unit, -1)
    g = first_to_owner(grad_one, b)
    q = second_to_owner(grad_two, c)
    raw_one, raw_two, squares = contract(u, g, h, q)
    sums = jnp.where(lax.broadcasted_iota(jnp.int32, squares.shape, 0) == 0, squares, signed)
    sums = sums + swap(sums, "c")
    for axis in ("y", "z", X):
        sums = total(sums, axis)
    width = 16 * unit
    energy_gap = sums[1, 0] / (count * 32 * 80.0 * jnp.sqrt(jnp.float32(width)))
    scale = jnp.sqrt(sums[0, 0] / (2.0 * width * width) + 1e-06)
    return (raw_one / scale, raw_two / scale, energy_gap)


def solution(mesh):
    split = Mesh(mesh.devices.reshape(4, 2, 4, 2, 2), AXES)
    in_specs = (
        P(DP, FSDP), P(DP, FSDP), P(None, DP, FSDP), P(FSDP, None), P(FSDP, None), P(FSDP),
    )
    out_specs = (P(FSDP, DP), P(FSDP, DP), P())
    return jax.shard_map(local, mesh=split, in_specs=in_specs, out_specs=out_specs, check_vma=False)
```

```python
import jax
import jax.numpy as jnp
from jax import lax
from jax.experimental import pallas as pl
from jax.experimental.pallas import tpu as pltpu
from jax.sharding import Mesh
from jax.sharding import PartitionSpec as P

STEPS = 4
AXES = ("y", "c", "z", "a", "b")
DP = ("y", "c")
ZA = ("z", "a")
FSDP = ("z", "a", "b")
X = ("a", "b")


def pick(value, index, dim):
    return lax.dynamic_index_in_dim(value, index, dim, keepdims=False)


def send(value, axis, step):
    count = lax.axis_size(axis)
    return lax.ppermute(value, axis, [(j, j ^ step) for j in range(count)])


def swap(value, axis):
    return send(value, axis, 1)


def from_all(value, axis):
    near = {step: send(value, axis, step) for step in (1, 3, 2)}
    return [value, near[1], near[2], near[3]]


def to_each(values, axis):
    near = {step: send(values[step], axis, step) for step in (1, 3, 2)}
    return [values[0], near[1], near[2], near[3]]


def total(value, axis):
    parts = from_all(value, axis)
    return (parts[0] + parts[1]) + (parts[2] + parts[3])


def relative(value, axis, dim):
    me = lax.axis_index(axis)
    return jnp.stack([pick(value, me ^ k, dim) for k in range(value.shape[dim])], axis=dim)


def wave(*values):
    return lax.optimization_barrier(values)


def halves(value):
    unit = value.shape[1] // 16
    parts = [value[:, k * unit : (k + 1) * unit] for k in range(16)]
    return (jnp.concatenate(parts[::2], axis=1), jnp.concatenate(parts[1::2], axis=1))


def copy_all(plan, refs, sems):
    copies = [
        pltpu.make_async_copy(source, target, sems.at[k]) for k, (source, target) in enumerate(plan)
    ]
    for copy in copies:
        copy.start()
    for copy in copies:
        copy.wait()


def place_first(*refs):
    pieces, out, sems = (refs[:8], refs[8], refs[9])
    copy_all([(piece, out.at[k]) for k, piece in enumerate(pieces)], refs, sems)


def place_second(place, *refs):
    pieces, out, sems = (refs[:8], refs[8], refs[9])
    y, z, a = (place[k] for k in range(3))
    part = out.shape[1] // 4
    plan = []
    for ka in range(2):
        for ky in range(4):
            rows = pl.ds(pl.multiple_of((y ^ ky) * part, part), part)
            for kz in range(4):
                plan.append((pieces[4 * ka + ky].at[kz], out.at[(z ^ kz) * 2 + (a ^ ka), rows]))
    copy_all(plan, refs, sems)


def assemble(kernel, pieces, shape, copies, scalars=()):
    memory = [pl.BlockSpec(memory_space=pltpu.SMEM)] * len(scalars)
    memory += [pl.BlockSpec(memory_space=pl.ANY)] * len(pieces)
    return pl.pallas_call(
        kernel,
        out_shape=pltpu.VMEM(shape, pieces[0].dtype),
        in_specs=memory,
        out_specs=pl.BlockSpec(memory_space=pltpu.VMEM),
        scratch_shapes=[pltpu.SemaphoreType.DMA((copies,))],
        compiler_params=pltpu.CompilerParams(vmem_limit_bytes=12 * 1024 * 1024),
    )(*scalars, *pieces)


def gather(first_weight, second_weight, start):
    b, c = lax.axis_index("b"), lax.axis_index("c")
    rows, cols = first_weight.shape
    part, unit = rows // 4, cols // 16
    y, z, a = (lax.axis_index(axis) for axis in ("y", "z", "a"))
    even, odd = halves(lax.dynamic_slice_in_dim(second_weight, y * part, part, 0))
    mine, theirs = (jnp.where(b == 0, even, odd), jnp.where(b == 0, odd, even))
    got = swap(theirs, "b")
    even, odd = halves(first_weight)
    w_own = jnp.where(c == 0, even, odd)
    s_own = jnp.where(c == b, mine, got)
    s_other = swap(s_own, "a")
    w_own, s_own, s_other, start = wave(w_own, s_own, s_other, start)
    s_own = {0: s_own, 1: send(s_own, "z", 1), 3: send(s_own, "z", 3)}
    s_other = {0: s_other, 1: send(s_other, "z", 1), 3: send(s_other, "z", 3)}
    w_own, s_own, s_other = wave(w_own, s_own, s_other)
    s_own[2], s_other[2] = (send(s_own[1], "z", 3), send(s_other[3], "z", 1))
    left, right = (jnp.stack([half[k] for k in range(4)]) for half in (s_own, s_other))
    w_own, left, right = wave(w_own, left, right)
    left, right = ({0: left}, {0: right})
    left[1], right[3] = (send(left[0], "y", 1), send(right[0], "y", 3))
    w_left, w_right = ({0: w_own}, {0: swap(w_own, "a")})
    w_left[1], w_left[3] = (send(w_own, "z", 1), send(w_own, "z", 3))
    left, right, w_left, w_right, start = wave(left, right, w_left, w_right, start)
    left[3], right[1] = (send(left[0], "y", 3), send(right[0], "y", 1))
    w_right[1], w_right[3] = (send(w_right[0], "z", 1), send(w_right[0], "z", 3))
    left, right, w_left, w_right = wave(left, right, w_left, w_right)
    left[2], right[2] = (send(left[1], "y", 3), send(right[3], "y", 1))
    w_left[2], w_right[2] = (send(w_left[1], "z", 3), send(w_right[3], "z", 1))
    shape = (8, rows, 8 * unit)
    pieces = [half[k] for k in range(4) for half in (w_left, w_right)]
    first = assemble(place_first, pieces, shape, 8)
    pieces = [half[k] for half in (left, right) for k in range(4)]
    place = jnp.stack([y, z, a]).astype(jnp.int32)
    second = assemble(place_second, pieces, shape, 32, (place,))
    return (first, second, start)


def to_groups(value):
    lead, rows, cols = value.shape
    part = rows // 8
    split = jnp.moveaxis(value.reshape(lead, 8, part, cols), 1, 0)
    got = lax.all_to_all(split, ZA, 0, 0, tiled=True).reshape(4, 2, lead, part, cols)
    got = relative(relative(got, "z", 0), "a", 1).reshape(8, lead, part, cols)
    own = jnp.transpose(got, (1, 2, 0, 3)).reshape(lead, part, 8 * cols)
    return by_index("c", own, swap(own, "c"), 1)


def by_index(axis, own, other, dim):
    first = lax.axis_index(axis) == 0
    return jnp.concatenate(
        [jnp.where(first, own, other), jnp.where(first, other, own)], axis=dim
    )


def spread(value, axis):
    count = lax.axis_size(axis)
    return lax.all_to_all(jnp.broadcast_to(value, (count, *value.shape)), axis, 0, 0, tiled=True)


def slope(values):
    sig = jax.nn.sigmoid(values)
    return sig * (1.0 + values * (1.0 - sig))


def share(part, axis, narrow):
    if narrow and axis == "b":
        part = part.astype(jnp.bfloat16)
    return part.astype(jnp.float32) + swap(part, axis).astype(jnp.float32)


def layer(inputs, block, axis, narrow):
    slices, depth, _ = block.shape
    split = inputs.reshape(inputs.shape[0], slices, depth)
    terms = jnp.einsum("rnk,nkm->nrm", split, block, preferred_element_type=jnp.float32)
    part = jnp.sum(terms.astype(jnp.bfloat16).astype(jnp.float32), axis=0)
    return share(part, axis, narrow)


def back(cotan, block, axis, narrow):
    flat = block.reshape(-1, block.shape[-1])
    part = lax.dot_general(
        cotan, flat, (((1,), (1,)), ((), ())), preferred_element_type=jnp.float32
    )
    return share(part, axis, narrow)


def one_pass(inputs, cotan, readout, first, second, narrow):
    pre_one = layer(inputs, first, "b", narrow)
    hidden = jax.nn.silu(pre_one).astype(jnp.bfloat16)
    pre_two = layer(hidden, second, "c", narrow)
    grad_two = (cotan[:, None] * readout[None, :] * slope(pre_two)).astype(jnp.bfloat16)
    grad_one = (back(grad_two, second, "b", narrow) * slope(pre_one)).astype(jnp.bfloat16)
    return (hidden, pre_two, grad_two, grad_one)


def products(u_ref, g_ref, h_ref, q_ref, one_ref, two_ref, sum_ref):
    one = jnp.dot(u_ref[...], g_ref[...], preferred_element_type=jnp.float32)
    one_ref[...] = one
    two = jnp.dot(h_ref[...], q_ref[...], preferred_element_type=jnp.float32)
    two_ref[...] = two
    sum_ref[...] = jnp.full(sum_ref.shape, jnp.sum(one * one) + jnp.sum(two * two))


def contract(u, g, h, q):
    tile = jax.ShapeDtypeStruct((u.shape[0], g.shape[1]), jnp.float32)
    return pl.pallas_call(
        products,
        out_shape=(tile, tile, jax.ShapeDtypeStruct((8, 128), jnp.float32)),
        compiler_params=pltpu.CompilerParams(vmem_limit_bytes=32 * 1024 * 1024),
    )(u, g, h, q)


def rows_to_owner(rows, hidden, c, b):
    count = rows.shape[0] // 2
    unit = rows.shape[1] // 8
    half = lambda value, at: pick(value.reshape(2, count, 4, 2, unit), at, 0)
    crossed = swap(half(hidden, 1 - c), "c")
    hidden_part = jnp.where(c == b, half(hidden, c), crossed)
    hidden_part = relative(relative(hidden_part, "z", 1), "a", 2)
    parts = jnp.concatenate([half(rows, c), hidden_part], axis=-1)
    parts = jnp.transpose(parts, (2, 1, 0, 3))
    pairs = jnp.stack([parts[0], swap(parts[1], "a")], axis=1)
    column = jnp.stack(to_each([pairs[k] for k in range(4)], "z"))
    plane = jnp.stack(from_all(column, "y"))
    return by_index("c", plane[None], swap(plane, "c")[None], 0)


def second_to_owner(grad, c):
    count = grad.shape[0] // 2
    unit = grad.shape[1] // 8
    mine = pick(grad.reshape(2, count, 4, 2, unit), c, 0)
    parts = jnp.transpose(relative(relative(mine, "y", 1), "c", 2), (2, 1, 0, 3))
    pairs = by_index("c", parts[0][:, None], swap(parts[1], "c")[:, None], 1)
    block = jnp.stack(to_each([pairs[k] for k in range(4)], "y"))
    near = from_all(block, X)
    row = jnp.stack([by_index("b", near[2 * k], near[2 * k + 1], -1) for k in range(2)])
    return jnp.stack(from_all(row, "z")).reshape(-1, 2 * unit)


def first_to_owner(grad, b):
    count = grad.shape[0] // 2
    unit = grad.shape[1] // 8
    mine = pick(grad.reshape(2, count, 4, 2, unit), b, 0)
    parts = jnp.transpose(relative(relative(mine, "y", 1), "c", 2), (2, 1, 0, 3))
    pairs = by_index("c", parts[0], swap(parts[1], "c"), -1)
    block = jnp.stack(to_each([pairs[k] for k in range(4)], "y"))
    column = jnp.stack(from_all(block, "z"))
    near = from_all(column, X)
    return jnp.stack(
        [by_index("b", near[2 * k][None], near[2 * k + 1][None], 0) for k in range(2)]
    ).reshape(-1, 2 * unit)


def local(data_samples, negative_start, langevin_noise, first_weight, second_weight, readout):
    c, b = lax.axis_index("c"), lax.axis_index("b")
    start = jnp.concatenate(
        [negative_start[None], langevin_noise, data_samples[None].astype(jnp.float32)]
    )
    first, second, start = gather(first_weight, second_weight, start)
    moved_in = to_groups(start)
    state, noise = (moved_in[0], moved_in[1:-1])
    data = moved_in[-1].astype(jnp.bfloat16)
    readout = spread(readout, ZA).reshape(-1)
    count = state.shape[0]
    ones = jnp.ones((count,), jnp.float32)
    for step in range(STEPS):
        inputs = state.astype(jnp.bfloat16)
        grad_one = one_pass(inputs, ones, readout, first, second, True)[3]
        state = state - 0.005 * back(grad_one, first, "c", True) + 0.1 * noise[step]
    rows = jnp.concatenate([data, state.astype(jnp.bfloat16)], axis=0)
    cotan = jnp.concatenate([ones, -ones])
    hidden, pre_two, grad_two, grad_one = one_pass(rows, cotan, readout, first, second, False)
    energies = jnp.sum(jax.nn.silu(pre_two) * readout[None, :], axis=1)
    signed = 0.5 * jnp.sum(cotan * energies)

    unit = rows.shape[1] // 8
    inner = rows_to_owner(rows, hidden, c, b)
    u = jnp.transpose(inner[..., :unit], (5, 3, 0, 2, 1, 4)).reshape(unit, -1)
    h = jnp.transpose(inner[..., unit:], (5, 2, 3, 1, 0, 4)).reshape(unit, -1)
    g = first_to_owner(grad_one, b)
    q = second_to_owner(grad_two, c)
    raw_one, raw_two, squares = contract(u, g, h, q)
    sums = jnp.where(lax.broadcasted_iota(jnp.int32, squares.shape, 0) == 0, squares, signed)
    sums = sums + swap(sums, "c")
    for axis in ("y", "z", X):
        sums = total(sums, axis)
    width = 16 * unit
    energy_gap = sums[1, 0] / (count * 32 * 80.0 * jnp.sqrt(jnp.float32(width)))
    scale = jnp.sqrt(sums[0, 0] / (2.0 * width * width) + 1e-06)
    return (raw_one / scale, raw_two / scale, energy_gap)


def solution(mesh):
    split = Mesh(mesh.devices.reshape(4, 2, 4, 2, 2), AXES)
    in_specs = (
        P(DP, FSDP), P(DP, FSDP), P(None, DP, FSDP), P(FSDP, None), P(FSDP, None), P(FSDP),
    )
    out_specs = (P(FSDP, DP), P(FSDP, DP), P())
    return jax.shard_map(local, mesh=split, in_specs=in_specs, out_specs=out_specs, check_vma=False)
```

```python
import jax
import jax.numpy as jnp
from jax import lax
from jax.experimental import pallas as pl
from jax.experimental.pallas import tpu as pltpu
from jax.sharding import Mesh
from jax.sharding import PartitionSpec as P

STEPS = 4
AXES = ("y", "c", "z", "a", "b")
DP = ("y", "c")
ZA = ("z", "a")
FSDP = ("z", "a", "b")
X = ("a", "b")
ROWS = (((0,), (0,)), ((), ()))


def pick(value, index, dim):
    return lax.dynamic_index_in_dim(value, index, dim, keepdims=False)


def send(value, axis, step):
    count = lax.axis_size(axis)
    return lax.ppermute(value, axis, [(j, j ^ step) for j in range(count)])


def swap(value, axis):
    return send(value, axis, 1)


def from_all(value, axis):
    near = {step: send(value, axis, step) for step in (1, 3, 2)}
    return [value, near[1], near[2], near[3]]


def from_all_large(value, axis):
    half = value.shape[0] // 2
    left, right = (value[:half], value[half:])
    left = jnp.stack([left, send(left, axis, 1)])
    right = jnp.stack([right, send(right, axis, 3)])
    left_far, right_far = (send(left, axis, 3), send(right, axis, 1))
    lefts = (left[0], left[1], left_far[1], left_far[0])
    rights = (right[0], right_far[0], right_far[1], right[1])
    return [jnp.concatenate(pair, axis=0) for pair in zip(lefts, rights)]


def to_each(values, axis):
    near = {step: send(values[step], axis, step) for step in (1, 3, 2)}
    return [values[0], near[1], near[2], near[3]]


def total(value, axis):
    parts = from_all(value, axis)
    return (parts[0] + parts[1]) + (parts[2] + parts[3])


def relative(value, axis, dim):
    me = lax.axis_index(axis)
    return jnp.stack([pick(value, me ^ k, dim) for k in range(value.shape[dim])], axis=dim)


def flat(place):
    return 4 * place[0] + 2 * place[1] + place[2]


def wave(*values):
    return lax.optimization_barrier(values)


def copy_all(plan, refs, sems):
    copies = [
        pltpu.make_async_copy(source, target, sems.at[k]) for k, (source, target) in enumerate(plan)
    ]
    for copy in copies:
        copy.start()
    for copy in copies:
        copy.wait()


def pick_columns(place, *refs):
    count = len(refs) // 2
    for k in range(count):
        refs[count + k][...] = refs[k][...]


def columns(weight, first_row, rows, parity, count):
    unit = weight.shape[1] // 16
    place = jnp.stack([first_row // rows, parity]).astype(jnp.int32)
    shape = jax.ShapeDtypeStruct((rows, 8 * unit), weight.dtype)
    source = lambda k: pl.BlockSpec(
        (rows, unit), lambda n, place: (place[0], 2 * n + (place[1] ^ k))
    )
    return pl.pallas_call(
        pick_columns,
        out_shape=(shape,) * count,
        grid_spec=pltpu.PrefetchScalarGridSpec(
            num_scalar_prefetch=1,
            grid=(8,),
            in_specs=[source(k) for k in range(count)],
            out_specs=(pl.BlockSpec((rows, unit), lambda n, place: (0, n)),) * count,
        ),
    )(place, *([weight] * count))


def place_first(*refs):
    pieces, out, sems = (refs[:8], refs[8], refs[9])
    copy_all([(piece, out.at[k]) for k, piece in enumerate(pieces)], refs, sems)


def place_second(place, *refs):
    pieces, out, sems = (refs[:8], refs[8], refs[9])
    y, z, a = (place[k] for k in range(3))
    part = out.shape[1] // 4
    plan = []
    for ka in range(2):
        for ky in range(4):
            rows = pl.ds(pl.multiple_of((y ^ ky) * part, part), part)
            for kz in range(4):
                plan.append((pieces[4 * ka + ky].at[kz], out.at[(z ^ kz) * 2 + (a ^ ka), rows]))
    copy_all(plan, refs, sems)


def assemble(kernel, pieces, shape, copies, scalars=()):
    memory = [pl.BlockSpec(memory_space=pltpu.SMEM)] * len(scalars)
    memory += [pl.BlockSpec(memory_space=pl.ANY)] * len(pieces)
    return pl.pallas_call(
        kernel,
        out_shape=pltpu.VMEM(shape, pieces[0].dtype),
        in_specs=memory,
        out_specs=pl.BlockSpec(memory_space=pltpu.VMEM),
        scratch_shapes=[pltpu.SemaphoreType.DMA((copies,))],
        compiler_params=pltpu.CompilerParams(vmem_limit_bytes=12 * 1024 * 1024),
    )(*scalars, *pieces)


def gather(first_weight, second_weight, arrays, readout):
    b, c = lax.axis_index("b"), lax.axis_index("c")
    rows, cols = first_weight.shape
    part, unit = rows // 4, cols // 16
    y, z, a = (lax.axis_index(axis) for axis in ("y", "z", "a"))
    same, other = columns(second_weight, y * part, part, c, 2)
    cross = ("c", "a", "b")
    pairs = [((i, j, i), (i, j, 1 - i)) for i in range(2) for j in range(2)]
    got = lax.ppermute(other, cross, [(flat(f), flat(t)) for f, t in pairs])
    pairs = [((i, j, i), (i, 1 - j, i)) for i in range(2) for j in range(2)]
    pairs += [((1 - i, j, i), (i, 1 - j, 1 - i)) for i in range(2) for j in range(2)]
    s_other = lax.ppermute(same, cross, [(flat(f), flat(t)) for f, t in pairs])
    same, first_weight = wave(same, first_weight)
    (w_own,) = columns(first_weight, 0, rows, c, 1)
    s_own = jnp.where(c == b, same, got)
    w_own, s_own, s_other, arrays, readout = wave(w_own, s_own, s_other, arrays, readout)
    w_across = swap(w_own, "a")
    start = start_blocks(arrays, readout)
    s_own = {0: s_own, 1: send(s_own, "z", 1), 3: send(s_own, "z", 3)}
    s_other = {0: s_other, 1: send(s_other, "z", 1), 3: send(s_other, "z", 3)}
    w_own, s_own, s_other, start = wave(w_own, s_own, s_other, start)
    start = to_groups(start, len(arrays))
    s_own[2], s_other[2] = (send(s_own[1], "z", 3), send(s_other[3], "z", 1))
    left, right = (jnp.stack([half[k] for k in range(4)]) for half in (s_own, s_other))
    w_own, left, right = wave(w_own, left, right)
    left, right = ({0: left}, {0: right})
    left[1], right[3] = (send(left[0], "y", 1), send(right[0], "y", 3))
    w_left, w_right = ({0: w_own}, {0: w_across})
    w_left[1], w_left[3] = (send(w_own, "z", 1), send(w_own, "z", 3))
    left, right, w_left, w_right = wave(left, right, w_left, w_right)
    left[3], right[1] = (send(left[0], "y", 3), send(right[0], "y", 1))
    w_right[1], w_right[3] = (send(w_right[0], "z", 1), send(w_right[0], "z", 3))
    left, right, w_left, w_right = wave(left, right, w_left, w_right)
    left[2], right[2] = (send(left[1], "y", 3), send(right[3], "y", 1))
    w_left[2], w_right[2] = (send(w_left[1], "z", 3), send(w_right[3], "z", 1))
    shape = (8, rows, 8 * unit)
    pieces = [half[k] for k in range(4) for half in (w_left, w_right)]
    first = assemble(place_first, pieces, shape, 8)
    pieces = [half[k] for half in (left, right) for k in range(4)]
    place = jnp.stack([y, z, a]).astype(jnp.int32)
    second = assemble(place_second, pieces, shape, 32, (place,))
    return (first, second, start)


def start_blocks(arrays, readout):
    blocks = []
    for value in arrays:
        rows, cols = value.shape
        blocks.append(value.reshape(8, rows // 8, cols).astype(jnp.float32))
    blocks.append(jnp.broadcast_to(readout, (8, 8, readout.shape[0])))
    return jnp.concatenate(blocks, axis=1)


def to_groups(start, lead):
    got = lax.all_to_all(start, ZA, 0, 0, tiled=True)
    count, cols = got.shape[1:]
    readout = got[:, count - 8].reshape(-1)
    got = got[:, : count - 8].reshape(4, 2, lead, -1, cols)
    part = got.shape[3]
    got = relative(relative(got, "z", 0), "a", 1).reshape(8, lead, part, cols)
    own = jnp.transpose(got, (1, 2, 0, 3)).reshape(lead, part, 8 * cols)
    return (by_index("c", own, swap(own, "c"), 1), readout)


def by_index(axis, own, other, dim):
    first = lax.axis_index(axis) == 0
    return jnp.concatenate(
        [jnp.where(first, own, other), jnp.where(first, other, own)], axis=dim
    )


def slope(values):
    sig = jax.nn.sigmoid(values)
    return sig * (1.0 + values * (1.0 - sig))


def share_scaled(part, axis):
    top = jnp.max(jnp.abs(part), axis=1, keepdims=True)
    power = jnp.ceil(jnp.log2(jnp.maximum(top, 1e-30)))
    scaled = (part * jnp.exp2(14.0 - power)).astype(jnp.float16)
    tail = jnp.broadcast_to(power, (part.shape[0], 128)).astype(jnp.float16)
    got = swap(jnp.concatenate([scaled, tail], axis=1), axis)
    other = got[:, :-128].astype(jnp.float32) * jnp.exp2(got[:, -1:].astype(jnp.float32) - 14.0)
    return scaled.astype(jnp.float32) * jnp.exp2(power - 14.0) + other


def share(part, axis, narrow):
    if axis == "b" and not narrow:
        return share_scaled(part, axis)
    if narrow:
        part = part.astype(jnp.bfloat16)
    return part.astype(jnp.float32) + swap(part, axis).astype(jnp.float32)


def layer(inputs, block, axis, narrow):
    slices, depth, _ = block.shape
    split = inputs.reshape(inputs.shape[0], slices, depth)
    terms = jnp.einsum("rnk,nkm->nrm", split, block, preferred_element_type=jnp.float32)
    part = jnp.sum(terms.astype(jnp.bfloat16).astype(jnp.float32), axis=0)
    return share(part, axis, narrow)


def back(cotan, block, axis, narrow):
    flat = block.reshape(-1, block.shape[-1])
    part = lax.dot_general(
        cotan, flat, (((1,), (1,)), ((), ())), preferred_element_type=jnp.float32
    )
    return share(part, axis, narrow)


def one_pass(inputs, cotan, readout, first, second, narrow):
    pre_one = layer(inputs, first, "b", narrow)
    hidden = jax.nn.silu(pre_one).astype(jnp.bfloat16)
    pre_two = layer(hidden, second, "c", narrow)
    grad_two = (cotan[:, None] * readout[None, :] * slope(pre_two)).astype(jnp.bfloat16)
    summed = back(grad_two, second, "b", narrow)
    if not narrow:
        summed, grad_two = wave(summed, grad_two)
    grad_one = (summed * slope(pre_one)).astype(jnp.bfloat16)
    return (hidden, pre_two, grad_two, grad_one)


def products(u_ref, g_ref, h_ref, q_ref, one_ref, two_ref, sum_ref):
    one = lax.dot_general(u_ref[...], g_ref[...], ROWS, preferred_element_type=jnp.float32)
    one_ref[...] = one
    two = lax.dot_general(h_ref[...], q_ref[...], ROWS, preferred_element_type=jnp.float32)
    two_ref[...] = two
    sum_ref[...] = jnp.full(sum_ref.shape, jnp.sum(one * one) + jnp.sum(two * two))


def contract(u, g, h, q):
    tile = jax.ShapeDtypeStruct((u.shape[1], g.shape[1]), jnp.float32)
    return pl.pallas_call(
        products,
        out_shape=(tile, tile, jax.ShapeDtypeStruct((8, 128), jnp.float32)),
        compiler_params=pltpu.CompilerParams(vmem_limit_bytes=16 * 1024 * 1024),
    )(u, g, h, q)


def rows_to_owner(rows, hidden, c, b):
    count = rows.shape[0] // 2
    unit = rows.shape[1] // 8
    half = lambda value, at: pick(value.reshape(2, count, 4, 2, unit), at, 0)
    crossed = swap(half(hidden, 1 - c), "c")
    hidden_part = jnp.where(c == b, half(hidden, c), crossed)
    hidden_part = relative(relative(hidden_part, "z", 1), "a", 2)
    parts = jnp.concatenate([half(rows, c), hidden_part], axis=-1)
    parts = jnp.transpose(parts, (2, 1, 0, 3))
    pairs = jnp.stack([parts[0], swap(parts[1], "a")], axis=1)
    column = jnp.stack(to_each([pairs[k] for k in range(4)], "z"))
    plane = jnp.stack(from_all(column, "y"))
    return by_index("c", plane[None], swap(plane, "c")[None], 0)


def grads_to_owner(grad_one, grad_two):
    b, c = lax.axis_index("b"), lax.axis_index("c")
    count = grad_one.shape[0] // 2
    unit = grad_one.shape[1] // 8
    split = lambda value, at: pick(value.reshape(2, count, 4, 2, unit), at, 0)
    mine = jnp.stack([split(grad_one, b), split(grad_two, c)])
    parts = jnp.transpose(relative(relative(mine, "y", 2), "c", 3), (3, 2, 0, 1, 4))
    pairs = by_index("c", parts[0][:, :, None], swap(parts[1], "c")[:, :, None], 2)
    block = jnp.stack(to_each([pairs[k] for k in range(4)], "y"))
    block_one = jnp.concatenate([block[:, 0, 0], block[:, 0, 1]], axis=-1)
    near = from_all(block[:, 1], X)
    row = jnp.stack([by_index("b", near[2 * k], near[2 * k + 1], -1) for k in range(2)])
    column = jnp.stack(from_all(block_one, "z"))
    q = jnp.stack(from_all_large(row, "z")).reshape(-1, 2 * unit)
    near = from_all_large(column, X)
    g = jnp.stack(
        [by_index("b", near[2 * k][None], near[2 * k + 1][None], 0) for k in range(2)]
    ).reshape(-1, 2 * unit)
    return (g, q)


def local(data_samples, negative_start, langevin_noise, first_weight, second_weight, readout):
    arrays = [negative_start, *(langevin_noise[k] for k in range(STEPS)), data_samples]
    first, second, start = gather(first_weight, second_weight, arrays, readout)
    moved_in, readout = start
    state, noise = (moved_in[0], moved_in[1:-1])
    data = moved_in[-1].astype(jnp.bfloat16)
    count = state.shape[0]
    ones = jnp.ones((count,), jnp.float32)
    for step in range(STEPS):
        inputs = state.astype(jnp.bfloat16)
        grad_one = one_pass(inputs, ones, readout, first, second, True)[3]
        state = state - 0.005 * back(grad_one, first, "c", True) + 0.1 * noise[step]
    rows = jnp.concatenate([data, state.astype(jnp.bfloat16)], axis=0)
    cotan = jnp.concatenate([ones, -ones])
    hidden, pre_two, grad_two, grad_one = one_pass(rows, cotan, readout, first, second, False)
    energies = jnp.sum(jax.nn.silu(pre_two) * readout[None, :], axis=1)
    signed = 0.5 * jnp.sum(cotan * energies)

    b, c = lax.axis_index("b"), lax.axis_index("c")
    unit = rows.shape[1] // 8
    inner = rows_to_owner(rows, hidden, c, b)
    u = jnp.transpose(inner[..., :unit], (3, 0, 2, 1, 4, 5)).reshape(-1, unit)
    h = jnp.transpose(inner[..., unit:], (2, 3, 1, 0, 4, 5)).reshape(-1, unit)
    g, q = grads_to_owner(grad_one, grad_two)
    raw_one, raw_two, squares = contract(u, g, h, q)
    sums = jnp.where(lax.broadcasted_iota(jnp.int32, squares.shape, 0) == 0, squares, signed)
    sums = sums + swap(sums, "c")
    for axis in ("y", "z", X):
        sums = total(sums, axis)
    width = 16 * unit
    energy_gap = sums[1, 0] / (count * 32 * 80.0 * jnp.sqrt(jnp.float32(width)))
    scale = jnp.sqrt(sums[0, 0] / (2.0 * width * width) + 1e-06)
    return (raw_one / scale, raw_two / scale, energy_gap)


def solution(mesh):
    split = Mesh(mesh.devices.reshape(4, 2, 4, 2, 2), AXES)
    in_specs = (
        P(DP, FSDP), P(DP, FSDP), P(None, DP, FSDP), P(FSDP, None), P(FSDP, None), P(FSDP),
    )
    out_specs = (P(FSDP, DP), P(FSDP, DP), P())
    return jax.shard_map(local, mesh=split, in_specs=in_specs, out_specs=out_specs, check_vma=False)
```

```python
import jax
import jax.numpy as jnp
from jax import lax
from jax.experimental import pallas as pl
from jax.experimental.pallas import tpu as pltpu
from jax.sharding import Mesh
from jax.sharding import PartitionSpec as P

STEPS = 4
AXES = ("y", "c", "z", "a", "b")
DP = ("y", "c")
ZA = ("z", "a")
FSDP = ("z", "a", "b")
X = ("a", "b")
ROWS = (((0,), (0,)), ((), ()))


def pick(value, index, dim):
    return lax.dynamic_index_in_dim(value, index, dim, keepdims=False)


def send(value, axis, step):
    count = lax.axis_size(axis)
    return lax.ppermute(value, axis, [(j, j ^ step) for j in range(count)])


def swap(value, axis):
    return send(value, axis, 1)


def from_all(value, axis):
    near = {step: send(value, axis, step) for step in (1, 3, 2)}
    return [value, near[1], near[2], near[3]]


def from_all_large(value, axis):
    half = value.shape[0] // 2
    left, right = (value[:half], value[half:])
    left = jnp.stack([left, send(left, axis, 1)])
    right = jnp.stack([right, send(right, axis, 3)])
    left_far, right_far = (send(left, axis, 3), send(right, axis, 1))
    lefts = (left[0], left[1], left_far[1], left_far[0])
    rights = (right[0], right_far[0], right_far[1], right[1])
    return [jnp.concatenate(pair, axis=0) for pair in zip(lefts, rights)]


def to_each(values, axis):
    near = {step: send(values[step], axis, step) for step in (1, 3, 2)}
    return [values[0], near[1], near[2], near[3]]


def total(value, axis):
    parts = from_all(value, axis)
    return (parts[0] + parts[1]) + (parts[2] + parts[3])


def relative(value, axis, dim):
    me = lax.axis_index(axis)
    return jnp.stack([pick(value, me ^ k, dim) for k in range(value.shape[dim])], axis=dim)


def flat(place):
    return 4 * place[0] + 2 * place[1] + place[2]


def wave(*values):
    return lax.optimization_barrier(values)


def copy_all(plan, refs, sems):
    copies = [
        pltpu.make_async_copy(source, target, sems.at[k]) for k, (source, target) in enumerate(plan)
    ]
    for copy in copies:
        copy.start()
    for copy in copies:
        copy.wait()


def pick_columns(place, weight, *outs):
    unit = weight.shape[1] // 16
    for k, out in enumerate(outs):
        for parity in range(2):

            @pl.when(place[1] == (parity ^ k))
            def _(out=out, parity=parity):
                for n in range(8):
                    at = (2 * n + parity) * unit
                    out[:, n * unit : (n + 1) * unit] = weight[:, at : at + unit]


def columns(weight, first_block, blocks, parity, count):
    part, cols = (weight.shape[0] // 4, weight.shape[1])
    place = jnp.stack([first_block, parity]).astype(jnp.int32)
    shape = jax.ShapeDtypeStruct((blocks * part, cols // 2), weight.dtype)
    return pl.pallas_call(
        pick_columns,
        out_shape=(shape,) * count,
        grid_spec=pltpu.PrefetchScalarGridSpec(
            num_scalar_prefetch=1,
            grid=(blocks,),
            in_specs=[pl.BlockSpec((part, cols), lambda n, place: (place[0] + n, 0))],
            out_specs=(pl.BlockSpec((part, cols // 2), lambda n, place: (n, 0)),) * count,
        ),
    )(place, weight)


def place_first(*refs):
    pieces, out, sems = (refs[:8], refs[8], refs[9])
    copy_all([(piece, out.at[k]) for k, piece in enumerate(pieces)], refs, sems)


def place_second(place, *refs):
    pieces, out, sems = (refs[:8], refs[8], refs[9])
    y, z, a = (place[k] for k in range(3))
    part = out.shape[1] // 4
    plan = []
    for ka in range(2):
        for ky in range(4):
            rows = pl.ds(pl.multiple_of((y ^ ky) * part, part), part)
            for kz in range(4):
                plan.append((pieces[4 * ka + ky].at[kz], out.at[(z ^ kz) * 2 + (a ^ ka), rows]))
    copy_all(plan, refs, sems)


def assemble(kernel, pieces, shape, copies, scalars=()):
    memory = [pl.BlockSpec(memory_space=pltpu.SMEM)] * len(scalars)
    memory += [pl.BlockSpec(memory_space=pl.ANY)] * len(pieces)
    return pl.pallas_call(
        kernel,
        out_shape=pltpu.VMEM(shape, pieces[0].dtype),
        in_specs=memory,
        out_specs=pl.BlockSpec(memory_space=pltpu.VMEM),
        scratch_shapes=[pltpu.SemaphoreType.DMA((copies,))],
        compiler_params=pltpu.CompilerParams(vmem_limit_bytes=12 * 1024 * 1024),
    )(*scalars, *pieces)


def gather(first_weight, second_weight, arrays, readout):
    b, c = lax.axis_index("b"), lax.axis_index("c")
    rows, cols = first_weight.shape
    part, unit = rows // 4, cols // 16
    y, z, a = (lax.axis_index(axis) for axis in ("y", "z", "a"))
    same, other = columns(second_weight, y, 1, c, 2)
    cross = ("c", "a", "b")
    pairs = [((i, j, i), (i, j, 1 - i)) for i in range(2) for j in range(2)]
    got = lax.ppermute(other, cross, [(flat(f), flat(t)) for f, t in pairs])
    pairs = [((i, j, i), (i, 1 - j, i)) for i in range(2) for j in range(2)]
    pairs += [((1 - i, j, i), (i, 1 - j, 1 - i)) for i in range(2) for j in range(2)]
    s_other = lax.ppermute(same, cross, [(flat(f), flat(t)) for f, t in pairs])
    same, first_weight = wave(same, first_weight)
    (w_own,) = columns(first_weight, 0, 4, c, 1)
    s_own = jnp.where(c == b, same, got)
    w_own, s_own, s_other, arrays, readout = wave(w_own, s_own, s_other, arrays, readout)
    w_across = swap(w_own, "a")
    start = start_blocks(arrays, readout)
    s_own = {0: s_own, 1: send(s_own, "z", 1), 3: send(s_own, "z", 3)}
    s_other = {0: s_other, 1: send(s_other, "z", 1), 3: send(s_other, "z", 3)}
    w_own, s_own, s_other, start = wave(w_own, s_own, s_other, start)
    start = to_groups(start, len(arrays))
    s_own[2], s_other[2] = (send(s_own[1], "z", 3), send(s_other[3], "z", 1))
    left, right = (jnp.stack([half[k] for k in range(4)]) for half in (s_own, s_other))
    w_own, left, right = wave(w_own, left, right)
    left, right = ({0: left}, {0: right})
    left[1], right[3] = (send(left[0], "y", 1), send(right[0], "y", 3))
    w_left, w_right = ({0: w_own}, {0: w_across})
    w_left[1], w_left[3] = (send(w_own, "z", 1), send(w_own, "z", 3))
    left, right = wave(left, right)
    w_left, w_right = wave(w_left, w_right)
    left[3], right[1] = (send(left[0], "y", 3), send(right[0], "y", 1))
    w_right[1], w_right[3] = (send(w_right[0], "z", 1), send(w_right[0], "z", 3))
    left, right = wave(left, right)
    w_left, w_right = wave(w_left, w_right)
    left[2], right[2] = (send(left[1], "y", 3), send(right[3], "y", 1))
    w_left[2], w_right[2] = (send(w_left[1], "z", 3), send(w_right[3], "z", 1))
    shape = (8, rows, 8 * unit)
    pieces = [half[k] for k in range(4) for half in (w_left, w_right)]
    first = assemble(place_first, pieces, shape, 8)
    pieces = [half[k] for half in (left, right) for k in range(4)]
    place = jnp.stack([y, z, a]).astype(jnp.int32)
    second = assemble(place_second, pieces, shape, 32, (place,))
    return (first, second, start)


def start_blocks(arrays, readout):
    blocks = []
    for value in arrays:
        rows, cols = value.shape
        blocks.append(value.reshape(8, rows // 8, cols).astype(jnp.float32))
    blocks.append(jnp.broadcast_to(readout, (8, 8, readout.shape[0])))
    return jnp.concatenate(blocks, axis=1)


def to_groups(start, lead):
    got = lax.all_to_all(start, ZA, 0, 0, tiled=True)
    count, cols = got.shape[1:]
    readout = got[:, count - 8].reshape(-1)
    got = got[:, : count - 8].reshape(4, 2, lead, -1, cols)
    part = got.shape[3]
    got = relative(relative(got, "z", 0), "a", 1).reshape(8, lead, part, cols)
    own = jnp.transpose(got, (1, 2, 0, 3)).reshape(lead, part, 8 * cols)
    return (by_index("c", own, swap(own, "c"), 1), readout)


def by_index(axis, own, other, dim):
    first = lax.axis_index(axis) == 0
    return jnp.concatenate(
        [jnp.where(first, own, other), jnp.where(first, other, own)], axis=dim
    )


def slope(values):
    sig = jax.nn.sigmoid(values)
    return sig * (1.0 + values * (1.0 - sig))


def share_scaled(part, axis):
    top = jnp.max(jnp.abs(part), axis=1, keepdims=True)
    power = jnp.ceil(jnp.log2(jnp.maximum(top, 1e-30)))
    scaled = (part * jnp.exp2(14.0 - power)).astype(jnp.float16)
    tail = jnp.broadcast_to(power, (part.shape[0], 128)).astype(jnp.float16)
    got = swap(jnp.concatenate([scaled, tail], axis=1), axis)
    other = got[:, :-128].astype(jnp.float32) * jnp.exp2(got[:, -1:].astype(jnp.float32) - 14.0)
    return scaled.astype(jnp.float32) * jnp.exp2(power - 14.0) + other


def share(part, axis, narrow):
    if axis == "b" and not narrow:
        return share_scaled(part, axis)
    if narrow:
        part = part.astype(jnp.bfloat16)
    return part.astype(jnp.float32) + swap(part, axis).astype(jnp.float32)


def layer(inputs, block, axis, narrow):
    slices, depth, _ = block.shape
    split = inputs.reshape(inputs.shape[0], slices, depth)
    terms = jnp.einsum("rnk,nkm->nrm", split, block, preferred_element_type=jnp.float32)
    part = jnp.sum(terms.astype(jnp.bfloat16).astype(jnp.float32), axis=0)
    return share(part, axis, narrow)


def back(cotan, block, axis, narrow):
    flat = block.reshape(-1, block.shape[-1])
    part = lax.dot_general(
        cotan, flat, (((1,), (1,)), ((), ())), preferred_element_type=jnp.float32
    )
    return share(part, axis, narrow)


def one_pass(inputs, cotan, readout, first, second, narrow):
    pre_one = layer(inputs, first, "b", narrow)
    hidden = jax.nn.silu(pre_one).astype(jnp.bfloat16)
    pre_two = layer(hidden, second, "c", narrow)
    grad_two = (cotan[:, None] * readout[None, :] * slope(pre_two)).astype(jnp.bfloat16)
    summed = back(grad_two, second, "b", narrow)
    if not narrow:
        summed, grad_two = wave(summed, grad_two)
    grad_one = (summed * slope(pre_one)).astype(jnp.bfloat16)
    return (hidden, pre_two, grad_two, grad_one)


def products(u_ref, g_ref, h_ref, q_ref, one_ref, two_ref, sum_ref):
    one = lax.dot_general(u_ref[...], g_ref[...], ROWS, preferred_element_type=jnp.float32)
    one_ref[...] = one
    two = lax.dot_general(h_ref[...], q_ref[...], ROWS, preferred_element_type=jnp.float32)
    two_ref[...] = two
    sum_ref[...] = jnp.full(sum_ref.shape, jnp.sum(one * one) + jnp.sum(two * two))


def contract(u, g, h, q):
    tile = jax.ShapeDtypeStruct((u.shape[1], g.shape[1]), jnp.float32)
    return pl.pallas_call(
        products,
        out_shape=(tile, tile, jax.ShapeDtypeStruct((8, 128), jnp.float32)),
        compiler_params=pltpu.CompilerParams(vmem_limit_bytes=10 * 1024 * 1024),
    )(u, g, h, q)


def rows_to_owner(rows, hidden, c, b):
    count = rows.shape[0] // 2
    unit = rows.shape[1] // 8
    half = lambda value, at: pick(value.reshape(2, count, 4, 2, unit), at, 0)
    crossed = swap(half(hidden, 1 - c), "c")
    hidden_part = jnp.where(c == b, half(hidden, c), crossed)
    hidden_part = relative(relative(hidden_part, "z", 1), "a", 2)
    parts = jnp.concatenate([half(rows, c), hidden_part], axis=-1)
    parts = jnp.transpose(parts, (2, 1, 0, 3))
    pairs = jnp.stack([parts[0], swap(parts[1], "a")], axis=1)
    column = jnp.stack(to_each([pairs[k] for k in range(4)], "z"))
    plane = jnp.stack(from_all(column, "y"))
    return by_index("c", plane[None], swap(plane, "c")[None], 0)


def grads_to_owner(grad_one, grad_two):
    b, c = lax.axis_index("b"), lax.axis_index("c")
    count = grad_one.shape[0] // 2
    unit = grad_one.shape[1] // 8
    split = lambda value, at: pick(value.reshape(2, count, 4, 2, unit), at, 0)
    mine = jnp.stack([split(grad_one, b), split(grad_two, c)])
    parts = jnp.transpose(relative(relative(mine, "y", 2), "c", 3), (3, 2, 0, 1, 4))
    pairs = by_index("c", parts[0][:, :, None], swap(parts[1], "c")[:, :, None], 2)
    block = jnp.stack(to_each([pairs[k] for k in range(4)], "y"))
    block_one = jnp.concatenate([block[:, 0, 0], block[:, 0, 1]], axis=-1)
    near = from_all(block[:, 1], X)
    row = jnp.stack([by_index("b", near[2 * k], near[2 * k + 1], -1) for k in range(2)])
    column = jnp.stack(from_all(block_one, "z"))
    q = jnp.stack(from_all_large(row, "z")).reshape(-1, 2 * unit)
    near = from_all_large(column, X)
    g = jnp.stack(
        [by_index("b", near[2 * k][None], near[2 * k + 1][None], 0) for k in range(2)]
    ).reshape(-1, 2 * unit)
    return (g, q)


def local(data_samples, negative_start, langevin_noise, first_weight, second_weight, readout):
    arrays = [negative_start, *(langevin_noise[k] for k in range(STEPS)), data_samples]
    first, second, start = gather(first_weight, second_weight, arrays, readout)
    moved_in, readout = start
    state, noise = (moved_in[0], moved_in[1:-1])
    data = moved_in[-1].astype(jnp.bfloat16)
    count = state.shape[0]
    ones = jnp.ones((count,), jnp.float32)
    for step in range(STEPS):
        inputs = state.astype(jnp.bfloat16)
        grad_one = one_pass(inputs, ones, readout, first, second, True)[3]
        state = state - 0.005 * back(grad_one, first, "c", True) + 0.1 * noise[step]
    rows = jnp.concatenate([data, state.astype(jnp.bfloat16)], axis=0)
    cotan = jnp.concatenate([ones, -ones])
    hidden, pre_two, grad_two, grad_one = one_pass(rows, cotan, readout, first, second, False)
    energies = jnp.sum(jax.nn.silu(pre_two) * readout[None, :], axis=1)
    signed = 0.5 * jnp.sum(cotan * energies)

    b, c = lax.axis_index("b"), lax.axis_index("c")
    unit = rows.shape[1] // 8
    inner = rows_to_owner(rows, hidden, c, b)
    u = jnp.transpose(inner[..., :unit], (3, 0, 2, 1, 4, 5)).reshape(-1, unit)
    h = jnp.transpose(inner[..., unit:], (2, 3, 1, 0, 4, 5)).reshape(-1, unit)
    g, q = grads_to_owner(grad_one, grad_two)
    raw_one, raw_two, squares = contract(u, g, h, q)
    sums = jnp.where(lax.broadcasted_iota(jnp.int32, squares.shape, 0) == 0, squares, signed)
    sums = sums + swap(sums, "c")
    for axis in ("y", "z", X):
        sums = total(sums, axis)
    width = 16 * unit
    energy_gap = sums[1, 0] / (count * 32 * 80.0 * jnp.sqrt(jnp.float32(width)))
    scale = jnp.sqrt(sums[0, 0] / (2.0 * width * width) + 1e-06)
    return (raw_one / scale, raw_two / scale, energy_gap)


def solution(mesh):
    split = Mesh(mesh.devices.reshape(4, 2, 4, 2, 2), AXES)
    in_specs = (
        P(DP, FSDP), P(DP, FSDP), P(None, DP, FSDP), P(FSDP, None), P(FSDP, None), P(FSDP),
    )
    out_specs = (P(FSDP, DP), P(FSDP, DP), P())
    return jax.shard_map(local, mesh=split, in_specs=in_specs, out_specs=out_specs, check_vma=False)
```

```python
import jax
import jax.numpy as jnp
from jax import lax
from jax.experimental import pallas as pl
from jax.experimental.pallas import tpu as pltpu
from jax.sharding import Mesh
from jax.sharding import PartitionSpec as P

STEPS = 4
AXES = ("y", "c", "z", "a", "b")
DP = ("y", "c")
ZA = ("z", "a")
FSDP = ("z", "a", "b")
X = ("a", "b")
ROWS = (((0,), (0,)), ((), ()))


def pick(value, index, dim):
    return lax.dynamic_index_in_dim(value, index, dim, keepdims=False)


def send(value, axis, step):
    count = lax.axis_size(axis)
    return lax.ppermute(value, axis, [(j, j ^ step) for j in range(count)])


def swap(value, axis):
    return send(value, axis, 1)


def from_all(value, axis):
    near = {step: send(value, axis, step) for step in (1, 3, 2)}
    return [value, near[1], near[2], near[3]]


def from_all_large(value, axis):
    half = value.shape[0] // 2
    left, right = (value[:half], value[half:])
    left = jnp.stack([left, send(left, axis, 1)])
    right = jnp.stack([right, send(right, axis, 3)])
    left_far, right_far = (send(left, axis, 3), send(right, axis, 1))
    lefts = (left[0], left[1], left_far[1], left_far[0])
    rights = (right[0], right_far[0], right_far[1], right[1])
    return [jnp.concatenate(pair, axis=0) for pair in zip(lefts, rights)]


def to_each(values, axis):
    near = {step: send(values[step], axis, step) for step in (1, 3, 2)}
    return [values[0], near[1], near[2], near[3]]


def total(value, axis):
    parts = from_all(value, axis)
    return (parts[0] + parts[1]) + (parts[2] + parts[3])


def relative(value, axis, dim):
    me = lax.axis_index(axis)
    return jnp.stack([pick(value, me ^ k, dim) for k in range(value.shape[dim])], axis=dim)


def flat(place):
    return 4 * place[0] + 2 * place[1] + place[2]


def wave(*values):
    return lax.optimization_barrier(values)


def copy_all(plan, refs, sems):
    copies = [
        pltpu.make_async_copy(source, target, sems.at[k]) for k, (source, target) in enumerate(plan)
    ]
    for copy in copies:
        copy.start()
    for copy in copies:
        copy.wait()


def pick_columns(place, weight, *outs):
    unit = weight.shape[1] // 16
    for k, out in enumerate(outs):
        for parity in range(2):

            @pl.when(place[1] == (parity ^ k))
            def _(out=out, parity=parity):
                for n in range(8):
                    at = (2 * n + parity) * unit
                    out[:, n * unit : (n + 1) * unit] = weight[:, at : at + unit]


def columns(weight, first_block, blocks, parity, count):
    part, cols = (weight.shape[0] // 4, weight.shape[1])
    place = jnp.stack([first_block, parity]).astype(jnp.int32)
    shape = jax.ShapeDtypeStruct((blocks * part, cols // 2), weight.dtype)
    return pl.pallas_call(
        pick_columns,
        out_shape=(shape,) * count,
        grid_spec=pltpu.PrefetchScalarGridSpec(
            num_scalar_prefetch=1,
            grid=(blocks,),
            in_specs=[pl.BlockSpec((part, cols), lambda n, place: (place[0] + n, 0))],
            out_specs=(pl.BlockSpec((part, cols // 2), lambda n, place: (n, 0)),) * count,
        ),
    )(place, weight)


def place_first(*refs):
    pieces, out, sems = (refs[:8], refs[8], refs[9])
    copy_all([(piece, out.at[k]) for k, piece in enumerate(pieces)], refs, sems)


def place_second(place, *refs):
    pieces, out, sems = (refs[:8], refs[8], refs[9])
    y, z, a = (place[k] for k in range(3))
    part = out.shape[1] // 4
    plan = []
    for ka in range(2):
        for ky in range(4):
            rows = pl.ds(pl.multiple_of((y ^ ky) * part, part), part)
            for kz in range(4):
                plan.append((pieces[4 * ka + ky].at[kz], out.at[(z ^ kz) * 2 + (a ^ ka), rows]))
    copy_all(plan, refs, sems)


def assemble(kernel, pieces, shape, copies, scalars=()):
    memory = [pl.BlockSpec(memory_space=pltpu.SMEM)] * len(scalars)
    memory += [pl.BlockSpec(memory_space=pl.ANY)] * len(pieces)
    return pl.pallas_call(
        kernel,
        out_shape=pltpu.VMEM(shape, pieces[0].dtype),
        in_specs=memory,
        out_specs=pl.BlockSpec(memory_space=pltpu.VMEM),
        scratch_shapes=[pltpu.SemaphoreType.DMA((copies,))],
        compiler_params=pltpu.CompilerParams(vmem_limit_bytes=12 * 1024 * 1024),
    )(*scalars, *pieces)


def gather(first_weight, second_weight, arrays, readout):
    b, c = lax.axis_index("b"), lax.axis_index("c")
    rows, cols = first_weight.shape
    part, unit = rows // 4, cols // 16
    y, z, a = (lax.axis_index(axis) for axis in ("y", "z", "a"))
    same, other = columns(second_weight, y, 1, c, 2)
    cross = ("c", "a", "b")
    pairs = [((i, j, i), (i, j, 1 - i)) for i in range(2) for j in range(2)]
    got = lax.ppermute(other, cross, [(flat(f), flat(t)) for f, t in pairs])
    pairs = [((i, j, i), (i, 1 - j, i)) for i in range(2) for j in range(2)]
    pairs += [((1 - i, j, i), (i, 1 - j, 1 - i)) for i in range(2) for j in range(2)]
    s_other = lax.ppermute(same, cross, [(flat(f), flat(t)) for f, t in pairs])
    same, first_weight = wave(same, first_weight)
    (w_own,) = columns(first_weight, 0, 4, c, 1)
    s_own = jnp.where(c == b, same, got)
    w_own, s_own, s_other, arrays, readout = wave(w_own, s_own, s_other, arrays, readout)
    w_across = swap(w_own, "a")
    start = start_blocks(arrays, readout)
    s_own = {0: s_own, 1: send(s_own, "z", 1), 3: send(s_own, "z", 3)}
    s_other = {0: s_other, 1: send(s_other, "z", 1), 3: send(s_other, "z", 3)}
    w_own, s_own, s_other, start = wave(w_own, s_own, s_other, start)
    start = to_groups(start, len(arrays))
    s_own[2], s_other[2] = (send(s_own[1], "z", 3), send(s_other[3], "z", 1))
    left, right = (jnp.stack([half[k] for k in range(4)]) for half in (s_own, s_other))
    left, right = wave(left, right)
    left, right = ({0: left}, {0: right})
    left[1], right[3] = (send(left[0], "y", 1), send(right[0], "y", 3))
    w_left, w_right = ({0: w_own}, {0: w_across})
    w_left[1], w_left[3] = (send(w_own, "z", 1), send(w_own, "z", 3))
    left, right = wave(left, right)
    w_left, w_right = wave(w_left, w_right)
    left[3], right[1] = (send(left[0], "y", 3), send(right[0], "y", 1))
    w_right[1], w_right[3] = (send(w_right[0], "z", 1), send(w_right[0], "z", 3))
    left, right = wave(left, right)
    w_left, w_right = wave(w_left, w_right)
    left[2], right[2] = (send(left[1], "y", 3), send(right[3], "y", 1))
    w_left[2], w_right[2] = (send(w_left[1], "z", 3), send(w_right[3], "z", 1))
    shape = (8, rows, 8 * unit)
    pieces = [half[k] for k in range(4) for half in (w_left, w_right)]
    first = assemble(place_first, pieces, shape, 8)
    pieces = [half[k] for half in (left, right) for k in range(4)]
    place = jnp.stack([y, z, a]).astype(jnp.int32)
    second = assemble(place_second, pieces, shape, 32, (place,))
    return (first, second, start)


def start_blocks(arrays, readout):
    blocks = []
    for value in arrays:
        rows, cols = value.shape
        blocks.append(value.reshape(8, rows // 8, cols).astype(jnp.float32))
    blocks.append(jnp.broadcast_to(readout, (8, 8, readout.shape[0])))
    return jnp.concatenate(blocks, axis=1)


def to_groups(start, lead):
    got = lax.all_to_all(start, ZA, 0, 0, tiled=True)
    count, cols = got.shape[1:]
    readout = got[:, count - 8].reshape(-1)
    got = got[:, : count - 8].reshape(4, 2, lead, -1, cols)
    part = got.shape[3]
    got = relative(relative(got, "z", 0), "a", 1).reshape(8, lead, part, cols)
    own = jnp.transpose(got, (1, 2, 0, 3)).reshape(lead, part, 8 * cols)
    return (by_index("c", own, swap(own, "c"), 1), readout)


def by_index(axis, own, other, dim):
    first = lax.axis_index(axis) == 0
    return jnp.concatenate(
        [jnp.where(first, own, other), jnp.where(first, other, own)], axis=dim
    )


def slope(values):
    sig = jax.nn.sigmoid(values)
    return sig * (1.0 + values * (1.0 - sig))


def share_scaled(part, axis):
    top = jnp.max(jnp.abs(part), axis=1, keepdims=True)
    power = jnp.ceil(jnp.log2(jnp.maximum(top, 1e-30)))
    scaled = (part * jnp.exp2(14.0 - power)).astype(jnp.float16)
    tail = jnp.broadcast_to(power, (part.shape[0], 128)).astype(jnp.float16)
    got = swap(jnp.concatenate([scaled, tail], axis=1), axis)
    other = got[:, :-128].astype(jnp.float32) * jnp.exp2(got[:, -1:].astype(jnp.float32) - 14.0)
    return scaled.astype(jnp.float32) * jnp.exp2(power - 14.0) + other


def share(part, axis, narrow):
    if axis == "b" and not narrow:
        return share_scaled(part, axis)
    if narrow:
        part = part.astype(jnp.bfloat16)
    return part.astype(jnp.float32) + swap(part, axis).astype(jnp.float32)


def layer(inputs, block, axis, narrow):
    slices, depth, _ = block.shape
    split = inputs.reshape(inputs.shape[0], slices, depth)
    terms = jnp.einsum("rnk,nkm->nrm", split, block, preferred_element_type=jnp.float32)
    part = jnp.sum(terms.astype(jnp.bfloat16).astype(jnp.float32), axis=0)
    return share(part, axis, narrow)


def back(cotan, block, axis, narrow):
    flat = block.reshape(-1, block.shape[-1])
    part = lax.dot_general(
        cotan, flat, (((1,), (1,)), ((), ())), preferred_element_type=jnp.float32
    )
    return share(part, axis, narrow)


def one_pass(inputs, cotan, readout, first, second, narrow):
    pre_one = layer(inputs, first, "b", narrow)
    hidden = jax.nn.silu(pre_one).astype(jnp.bfloat16)
    pre_two = layer(hidden, second, "c", narrow)
    grad_two = (cotan[:, None] * readout[None, :] * slope(pre_two)).astype(jnp.bfloat16)
    summed = back(grad_two, second, "b", narrow)
    if not narrow:
        summed, grad_two = wave(summed, grad_two)
    grad_one = (summed * slope(pre_one)).astype(jnp.bfloat16)
    return (hidden, pre_two, grad_two, grad_one)


def products(u_ref, g_ref, h_ref, q_ref, one_ref, two_ref, sum_ref):
    one = lax.dot_general(u_ref[...], g_ref[...], ROWS, preferred_element_type=jnp.float32)
    one_ref[...] = one
    two = lax.dot_general(h_ref[...], q_ref[...], ROWS, preferred_element_type=jnp.float32)
    two_ref[...] = two
    sum_ref[...] = jnp.full(sum_ref.shape, jnp.sum(one * one) + jnp.sum(two * two))


def contract(u, g, h, q):
    tile = jax.ShapeDtypeStruct((u.shape[1], g.shape[1]), jnp.float32)
    return pl.pallas_call(
        products,
        out_shape=(tile, tile, jax.ShapeDtypeStruct((8, 128), jnp.float32)),
        compiler_params=pltpu.CompilerParams(vmem_limit_bytes=10 * 1024 * 1024),
    )(u, g, h, q)


def rows_to_owner(rows, hidden, c, b):
    count = rows.shape[0] // 2
    unit = rows.shape[1] // 8
    half = lambda value, at: pick(value.reshape(2, count, 4, 2, unit), at, 0)
    crossed = swap(half(hidden, 1 - c), "c")
    hidden_part = jnp.where(c == b, half(hidden, c), crossed)
    hidden_part = relative(relative(hidden_part, "z", 1), "a", 2)
    parts = jnp.concatenate([half(rows, c), hidden_part], axis=-1)
    parts = jnp.transpose(parts, (2, 1, 0, 3))
    pairs = jnp.stack([parts[0], swap(parts[1], "a")], axis=1)
    column = jnp.stack(to_each([pairs[k] for k in range(4)], "z"))
    plane = jnp.stack(from_all(column, "y"))
    return by_index("c", plane[None], swap(plane, "c")[None], 0)


def grads_to_owner(grad_one, grad_two):
    b, c = lax.axis_index("b"), lax.axis_index("c")
    count = grad_one.shape[0] // 2
    unit = grad_one.shape[1] // 8
    split = lambda value, at: pick(value.reshape(2, count, 4, 2, unit), at, 0)
    mine = jnp.stack([split(grad_one, b), split(grad_two, c)])
    parts = jnp.transpose(relative(relative(mine, "y", 2), "c", 3), (3, 2, 0, 1, 4))
    pairs = by_index("c", parts[0][:, :, None], swap(parts[1], "c")[:, :, None], 2)
    block = jnp.stack(to_each([pairs[k] for k in range(4)], "y"))
    block_one = jnp.concatenate([block[:, 0, 0], block[:, 0, 1]], axis=-1)
    near = from_all(block[:, 1], X)
    row = jnp.stack([by_index("b", near[2 * k], near[2 * k + 1], -1) for k in range(2)])
    column = jnp.stack(from_all(block_one, "z"))
    q = jnp.stack(from_all_large(row, "z")).reshape(-1, 2 * unit)
    near = from_all_large(column, X)
    g = jnp.stack(
        [by_index("b", near[2 * k][None], near[2 * k + 1][None], 0) for k in range(2)]
    ).reshape(-1, 2 * unit)
    return (g, q)


def local(data_samples, negative_start, langevin_noise, first_weight, second_weight, readout):
    arrays = [negative_start, *(langevin_noise[k] for k in range(STEPS)), data_samples]
    first, second, start = gather(first_weight, second_weight, arrays, readout)
    moved_in, readout = start
    state, noise = (moved_in[0], moved_in[1:-1])
    data = moved_in[-1].astype(jnp.bfloat16)
    count = state.shape[0]
    ones = jnp.ones((count,), jnp.float32)
    for step in range(STEPS):
        inputs = state.astype(jnp.bfloat16)
        grad_one = one_pass(inputs, ones, readout, first, second, True)[3]
        state = state - 0.005 * back(grad_one, first, "c", True) + 0.1 * noise[step]
    rows = jnp.concatenate([data, state.astype(jnp.bfloat16)], axis=0)
    cotan = jnp.concatenate([ones, -ones])
    hidden, pre_two, grad_two, grad_one = one_pass(rows, cotan, readout, first, second, False)
    energies = jnp.sum(jax.nn.silu(pre_two) * readout[None, :], axis=1)
    signed = 0.5 * jnp.sum(cotan * energies)

    b, c = lax.axis_index("b"), lax.axis_index("c")
    unit = rows.shape[1] // 8
    inner = rows_to_owner(rows, hidden, c, b)
    u = jnp.transpose(inner[..., :unit], (3, 0, 2, 1, 4, 5)).reshape(-1, unit)
    h = jnp.transpose(inner[..., unit:], (2, 3, 1, 0, 4, 5)).reshape(-1, unit)
    g, q = grads_to_owner(grad_one, grad_two)
    raw_one, raw_two, squares = contract(u, g, h, q)
    sums = jnp.where(lax.broadcasted_iota(jnp.int32, squares.shape, 0) == 0, squares, signed)
    sums = sums + swap(sums, "c")
    for axis in ("y", "z", X):
        sums = total(sums, axis)
    width = 16 * unit
    energy_gap = sums[1, 0] / (count * 32 * 80.0 * jnp.sqrt(jnp.float32(width)))
    scale = jnp.sqrt(sums[0, 0] / (2.0 * width * width) + 1e-06)
    return (raw_one / scale, raw_two / scale, energy_gap)


def solution(mesh):
    split = Mesh(mesh.devices.reshape(4, 2, 4, 2, 2), AXES)
    in_specs = (
        P(DP, FSDP), P(DP, FSDP), P(None, DP, FSDP), P(FSDP, None), P(FSDP, None), P(FSDP),
    )
    out_specs = (P(FSDP, DP), P(FSDP, DP), P())
    return jax.shard_map(local, mesh=split, in_specs=in_specs, out_specs=out_specs, check_vma=False)
```
